128 devices in a mesh: seq: 32 (over x, y, core), head: 4 (over z).
Axes of the slice: x: 4, y: 4, z: 4, core: 2. Of those that a mesh axis runs over, the one named last changes fastest.
Arguments:
- queries: bfloat16 [49152, 4096], P('seq', 'head'), may hold values from -4 to 4
- keys: bfloat16 [49152, 4096], P('seq', 'head'), may hold values from -4 to 4
- values: bfloat16 [49152, 4096], P('seq', 'head'), may hold values from -90 to 90, as said below
- out_grad: bfloat16 [49152, 4096], P('seq', 'head'), may hold values from -4 to 4
Outputs:
- result: bfloat16 [49152, 4096], P('seq', 'head')
- q_grad: bfloat16 [49152, 4096], P('seq', 'head')
- k_grad: bfloat16 [49152, 4096], P('seq', 'head')
- v_grad: bfloat16 [49152, 4096], P('seq', 'head')
The draws below stay inside these ranges and needn't reach their ends.
Inputs may be any that keep to these rules, and one draw needn't show every extreme that they name: Real values of varying scale over tokens and features.
All inputs are finite; a program needn't handle non-finite values.
Results may differ from the reference program's by a relative error of at most 0.006.
Values sent between devices are 32-bit elements; how exact they have to be, the bound alone decides.
A program may use at most 192 MiB of HBM per device.

```python
import jax
import jax.numpy as jnp
from jax import lax

NH = 32
HD = 128
GROUP = 128
TOKENS = 49152


def draw_values(key, part):
    key = jax.random.fold_in(key, 11)
    key_base, key_chan, key_tok = jax.random.split(key, 3)
    head_pos = (jnp.arange(NH * HD) // HD).astype(jnp.float32) / (NH - 1)
    channel = jnp.exp(jax.random.uniform(key_chan, (NH * HD,), jnp.float32, jnp.log(0.3), jnp.log(3.0)))
    token = jnp.exp(jax.random.uniform(key_tok, (TOKENS, 1), jnp.float32, jnp.log(0.3), jnp.log(3.0)))
    base = jnp.clip(jax.random.normal(key_base, (TOKENS, NH * HD), jnp.float32), -4.0, 4.0)
    rise = 3.0 ** head_pos / 1.7320508
    return (base * rise * channel * token).astype(jnp.bfloat16)


def block_levels(own_key, dims, pieces, smallest, top_value):
    def one(axis_at, parts):
        heights = jax.random.uniform(jax.random.fold_in(jax.random.fold_in(own_key, 6), axis_at), (parts,), jnp.float32, smallest / len(pieces), top_value / len(pieces))
        return jnp.repeat(jnp.exp(heights), dims[axis_at] // parts).reshape((-1,) + (1,) * (len(dims) - axis_at - 1))

    gain = one(*pieces[0])
    for cut in pieces[1:]:
        gain = gain * one(*cut)
    return gain


def noise(stream_key, extent, deviation, most, pieces=(), dtype=jnp.bfloat16):
    drawn = jax.random.normal(stream_key, extent, jnp.float32) * deviation
    if len(pieces) > 0:
        drawn = block_levels(stream_key, extent, pieces, -0.22, 0.18) * drawn
    return jnp.clip(drawn, min=-most, max=most).astype(dtype)


def setup_inputs(seed: int = 0) -> dict:
    arg_keys = jax.random.split(jax.random.key(seed), 5)
    queries = noise(arg_keys[0], (TOKENS, NH * HD), 1.0, 4.0, ((0, 32), (1, 4)))
    keys = noise(arg_keys[1], (TOKENS, NH * HD), 1.0, 4.0, ((0, 32), (1, 4)))
    values = draw_values(jax.random.fold_in(arg_keys[4], 71), 0)
    out_grad = noise(arg_keys[3], (TOKENS, NH * HD), 1.0, 4.0, ((0, 32), (1, 4)))
    return {"queries": queries, "keys": keys, "values": values, "out_grad": out_grad}


epsilon = 1e-05

def contract(form, first_part, second_part):
    return jnp.einsum(form, first_part.astype(jnp.float32), second_part.astype(jnp.float32), precision=lax.Precision.HIGHEST)

def reference(queries, keys, values, out_grad):
    factor = HD ** (-0.5)
    width_all = NH * HD
    group_count = TOKENS // GROUP
    shape_four = (group_count, GROUP, NH, HD)
    q_groups = queries.reshape(shape_four)
    k_groups = keys.reshape(shape_four)
    v_groups = values.reshape(shape_four)
    g_groups = out_grad.reshape(shape_four)
    causal = lax.broadcasted_iota(jnp.int32, (GROUP, GROUP), 0) >= lax.broadcasted_iota(jnp.int32, (GROUP, GROUP), 1)

    def forward_step(kv_state, inputs):
        q_part, k_part, v_part, g_part = inputs
        scores = contract('ihd,jhd->hij', q_part, k_part) * factor
        weights = jnp.where(causal, scores, 0.0).astype(jnp.bfloat16)
        state_bf = kv_state.astype(jnp.bfloat16)
        out_raw = contract('hij,jhe->ihe', weights, v_part) + factor * contract('ihd,hde->ihe', q_part, state_bf)
        recip = lax.rsqrt(lax.optimization_barrier(jnp.sum(out_raw * out_raw, axis=(1, 2))) / width_all + epsilon)
        result = (out_raw * recip[:, None, None]).astype(jnp.bfloat16)
        grad_f = g_part.astype(jnp.float32)
        inner = lax.optimization_barrier(jnp.sum(grad_f * out_raw, axis=(1, 2)))
        grad_raw = recip[:, None, None] * grad_f - (recip ** 3 * inner / width_all)[:, None, None] * out_raw
        grad_bf = grad_raw.astype(jnp.bfloat16)
        dscore = jnp.where(causal, factor * contract('ihe,jhe->hij', grad_bf, v_part), 0.0).astype(jnp.bfloat16)
        q_grad = contract('hij,jhd->ihd', dscore, k_part) + factor * contract('ihe,hde->ihd', grad_bf, state_bf)
        new_state = kv_state + contract('jhd,jhe->hde', k_part, v_part)
        return (new_state, (result, q_grad.astype(jnp.bfloat16), grad_bf))
    start_state = jnp.zeros((NH, HD, HD), jnp.float32)
    unused, outputs = lax.scan(forward_step, start_state, (q_groups, k_groups, v_groups, g_groups))
    result, q_grad, grad_groups = outputs

    def backward_step(grad_state, inputs):
        q_part, k_part, v_part, grad_bf = inputs
        scores = contract('ihd,jhd->hij', q_part, k_part) * factor
        weights = jnp.where(causal, scores, 0.0).astype(jnp.bfloat16)
        dscore = jnp.where(causal, factor * contract('ihe,jhe->hij', grad_bf, v_part), 0.0).astype(jnp.bfloat16)
        suffix_bf = grad_state.astype(jnp.bfloat16)
        k_grad = contract('hij,ihd->jhd', dscore, q_part) + contract('jhe,hde->jhd', v_part, suffix_bf)
        v_grad = contract('hij,ihe->jhe', weights, grad_bf) + contract('jhd,hde->jhe', k_part, suffix_bf)
        new_state = grad_state + factor * contract('ihd,ihe->hde', q_part, grad_bf)
        return (new_state, (k_grad.astype(jnp.bfloat16), v_grad.astype(jnp.bfloat16)))
    unused_two, grads = lax.scan(backward_step, start_state, (q_groups, k_groups, v_groups, grad_groups), reverse=True)
    k_grad, v_grad = grads
    flat = (TOKENS, width_all)
    return (result.reshape(flat), q_grad.reshape(flat), k_grad.reshape(flat), v_grad.reshape(flat))
```

```python
import functools

import jax
import jax.numpy as jnp
from jax import lax
from jax.experimental import pallas as pl
from jax.experimental.pallas import tpu as pltpu
from jax.sharding import PartitionSpec as P

HD = 128
CHUNK = 256
SUB = 128
STAGES = 2
EPSILON = 1e-05

MESH = pl.DeviceIdType.MESH
F32 = jnp.float32
BF16 = jnp.bfloat16
MIB = 1 << 20


def nn(a, b):
    return lax.dot_general(a, b, (((1,), (0,)), ((), ())), preferred_element_type=F32)


def nt(a, b):
    return lax.dot_general(a, b, (((1,), (1,)), ((), ())), preferred_element_type=F32)


def tn(a, b):
    return lax.dot_general(a, b, (((0,), (0,)), ((), ())), preferred_element_type=F32)


def tile(ref, chunk, head):
    row, col = chunk * CHUNK, head * HD
    if not isinstance(row, int):
        row = pl.multiple_of(row, CHUNK)
    if not isinstance(col, int):
        col = pl.multiple_of(col, HD)
    return ref.at[pl.ds(row, CHUNK), pl.ds(col, HD)]


class Scan:
    def __init__(self, refs, heads, backward):
        self.tot, self.pin, self.mine, self.got, self.pre, self.back, self.snd, self.carry = refs[:8]
        self.pair_s, self.pair_r, self.gat_s, self.gat_r, self.ret_s, self.ret_r, self.fin_s, self.fin_r = refs[8:]
        self.half = heads // 2
        self.width = self.half // STAGES
        self.backward = backward
        self.chips = lax.axis_size("seq") // 2
        seq = lax.axis_index("seq")
        self.core = seq % 2
        self.chip = seq // 2
        self.partner = self.chip * 2 + 1 - self.core
        self.later = (1 - self.core if backward else self.core).astype(F32)

    def own(self, stage):
        return self.core * self.half + stage * self.width

    def other(self, stage):
        return (1 - self.core) * self.half + stage * self.width

    def copy(self, src, dst, send, recv, seq):
        return pltpu.make_async_remote_copy(
            src_ref=src, dst_ref=dst, send_sem=send, recv_sem=recv, device_id={"seq": seq}, device_id_type=MESH
        )

    def pair(self, stage):
        return self.copy(
            self.tot.at[pl.ds(self.other(stage), self.width)],
            self.pin.at[stage],
            self.pair_s.at[stage],
            self.pair_r.at[stage],
            self.partner,
        )

    def gather(self, stage, step):
        chip = (self.chip + step) % self.chips
        return self.copy(
            self.mine.at[stage, chip],
            self.got.at[stage, self.chip],
            self.gat_s.at[stage, step],
            self.gat_r.at[stage, step],
            chip * 2 + self.core,
        )

    def give(self, stage, step):
        chip = (self.chip + step) % self.chips
        return self.copy(
            self.pre.at[stage, chip],
            self.back.at[stage, self.chip],
            self.ret_s.at[stage, step],
            self.ret_r.at[stage, step],
            chip * 2 + self.core,
        )

    def finish(self, stage):
        return self.copy(
            self.snd.at[stage],
            self.carry.at[pl.ds(self.own(stage), self.width)],
            self.fin_s.at[stage],
            self.fin_r.at[stage],
            self.partner,
        )

    def add_pair(self, stage):
        self.pair(stage).wait_recv()
        total = self.tot[pl.ds(self.own(stage), self.width)] + self.pin[stage]
        self.mine[stage] = total.reshape(self.mine.shape[1:])
        for step in range(1, self.chips):
            self.gather(stage, step).start()
        self.got[stage, self.chip] = self.mine[stage, self.chip]

    def add_chips(self, stage):
        for step in range(1, self.chips):
            self.gather(stage, step).wait_recv()
        order = range(self.chips)
        total = jnp.zeros(self.got.shape[2:], F32)
        for chip in reversed(order) if self.backward else order:
            self.pre[stage, chip] = total
            total = total + self.got[stage, chip]
        for step in range(1, self.chips):
            self.give(stage, step).start()
        self.back[stage, self.chip] = self.pre[stage, self.chip]

    def hand_over(self, stage):
        for step in range(1, self.chips):
            self.give(stage, step).wait_recv()
        before = self.back[stage].reshape((self.width, HD, HD))
        own = pl.ds(self.own(stage), self.width)
        self.snd[stage] = before + (1.0 - self.later) * self.tot[own]
        self.finish(stage).start()
        self.carry[own] = before + self.later * self.pin[stage]

    def arrive(self, stage):
        self.finish(stage).wait_recv()

    def drain(self):
        for stage in range(STAGES):
            self.pair(stage).wait_send()
            self.finish(stage).wait_send()
            for step in range(1, self.chips):
                self.gather(stage, step).wait_send()
                self.give(stage, step).wait_send()


def scan_scratch(heads, chips):
    half = heads // 2
    width = half // STAGES
    rows = width * HD // chips
    dma = pltpu.SemaphoreType.DMA
    return [
        pltpu.VMEM((heads, HD, HD), F32),
        pltpu.VMEM((STAGES, width, HD, HD), F32),
        pltpu.VMEM((STAGES, chips, rows, HD), F32),
        pltpu.VMEM((STAGES, chips, rows, HD), F32),
        pltpu.VMEM((STAGES, chips, rows, HD), F32),
        pltpu.VMEM((STAGES, chips, rows, HD), F32),
        pltpu.VMEM((STAGES, width, HD, HD), F32),
        pltpu.VMEM((heads, HD, HD), F32),
        dma((STAGES,)),
        dma((STAGES,)),
        dma((STAGES, chips)),
        dma((STAGES, chips)),
        dma((STAGES, chips)),
        dma((STAGES, chips)),
        dma((STAGES,)),
        dma((STAGES,)),
    ]


SCAN_REFS = 16


def split(x):
    high = x.astype(BF16)
    return high, (x - high.astype(F32)).astype(BF16)


def main_kernel(q_hbm, k_hbm, v_hbm, g_hbm, res, qg, kp, vp, k, v, sfx, *scratch):
    q, g, w, pre, pre_bf, norm, norm_in, in_sem, norm_s, norm_r = scratch[:10]
    fwd_refs = scratch[10 : 10 + SCAN_REFS]
    bwd_refs = scratch[10 + SCAN_REFS :]
    out = vp
    rows, width = q.shape
    heads, chunks = width // HD, rows // CHUNK
    factor = HD ** (-0.5)
    heads_all = heads * lax.axis_size("head")
    zs = lax.axis_size("head")
    z = lax.axis_index("head")
    forward = Scan(fwd_refs, heads, False)
    backward = Scan(bwd_refs, heads, True)
    seq, core, chip, chips = lax.axis_index("seq"), forward.core, forward.chip, forward.chips
    per = forward.width

    order = []
    for stage in range(STAGES):
        order += [forward.other(stage), forward.own(stage)]

    def load(which, part):
        src, dst = ((k_hbm, k), (v_hbm, v), (q_hbm, q), (g_hbm, g))[which]
        cols = pl.ds(pl.multiple_of(order[part] * HD, HD), per * HD)
        return pltpu.make_async_copy(src.at[:, cols], dst.at[:, cols], in_sem.at[which, part])

    for part in range(2 * STAGES):
        load(0, part).start()
        load(1, part).start()
    for part in range(2 * STAGES):
        load(2, part).start()
    for part in range(2 * STAGES):
        load(3, part).start()

    barrier = pltpu.get_barrier_semaphore()
    pl.semaphore_signal(barrier, inc=1, device_id={"seq": forward.partner}, device_id_type=MESH)
    for step in range(1, chips):
        pl.semaphore_signal(
            barrier, inc=1, device_id={"seq": ((chip + step) % chips) * 2 + core}, device_id_type=MESH
        )
    for step in range(1, zs):
        pl.semaphore_signal(barrier, inc=1, device_id={"head": (z + step) % zs}, device_id_type=MESH)

    def states(left, right, scan, first, chunk_order):
        def one(i, _):
            head = first + i
            total = jnp.zeros((HD, HD), F32)
            for c in chunk_order:
                pre[head, c] = total
                total = total + tn(tile(left, c, head)[...], tile(right, c, head)[...])
            scan.tot[head] = total
            return 0

        lax.fori_loop(0, per, one, 0)

    up, down = list(range(chunks)), list(reversed(range(chunks)))

    def kv(part):
        load(0, part).wait()
        load(1, part).wait()
        states(k, v, forward, order[part], up)

    row_at = lax.broadcasted_iota(jnp.int32, (SUB, SUB), 0)
    col_at = lax.broadcasted_iota(jnp.int32, (SUB, SUB), 1)
    causal = row_at >= col_at

    def masked(x):
        lines = []
        blocks = CHUNK // SUB
        for i in range(blocks):
            line = []
            for j in range(blocks):
                block = x[i * SUB : (i + 1) * SUB, j * SUB : (j + 1) * SUB] * factor
                if j > i:
                    line.append(jnp.zeros((SUB, SUB), BF16))
                elif j == i:
                    line.append(jnp.where(causal, block, 0.0).astype(BF16))
                else:
                    line.append(block.astype(BF16))
            lines.append(jnp.concatenate(line, axis=1))
        return jnp.concatenate(lines, axis=0)

    def local_forward(low, high):
        def one(head, _):
            for c in range(chunks):
                weights = masked(nt(tile(q, c, head)[...], tile(k, c, head)[...]))
                w[head, c] = weights
                tile(out, c, head)[...] = nn(weights, tile(v, c, head)[...])
            return 0

        lax.fori_loop(low, high, one, 0)

    kv(0)
    pl.semaphore_wait(barrier, chips - 1 + zs)
    forward.pair(0).start()
    kv(1)
    kv(2)
    forward.pair(1).start()
    forward.add_pair(0)
    kv(3)
    forward.add_pair(1)
    for part in range(2 * STAGES):
        load(2, part).wait()
    local_forward(0, heads // 2)
    forward.add_chips(0)
    forward.add_chips(1)
    for part in range(2 * STAGES):
        load(3, part).wait()
    local_forward(heads // 2, heads - 1)
    forward.hand_over(0)
    forward.hand_over(1)
    local_forward(heads - 1, heads)
    forward.arrive(0)
    forward.arrive(1)

    picks = lax.broadcasted_iota(jnp.int32, (8, 4 * HD), 0) // 4 == lax.broadcasted_iota(
        jnp.int32, (8, 4 * HD), 1
    ) // (2 * HD)
    picks = jnp.where(picks, 1.0, 0.0).astype(BF16)

    def norm_copy(c, step):
        return pltpu.make_async_remote_copy(
            src_ref=norm.at[c],
            dst_ref=norm_in.at[step - 1, c],
            send_sem=norm_s.at[step - 1, c],
            recv_sem=norm_r.at[step - 1, c],
            device_id={"head": (z + step) % zs},
            device_id_type=MESH,
        )

    def outputs(i, _):
        c = chunks - 1 - i
        squares = jnp.zeros((CHUNK, HD), F32)
        inner = jnp.zeros((CHUNK, HD), F32)
        for head in range(heads):
            state = (forward.carry[head] + pre[head, c]).astype(BF16)
            pre_bf[head, c] = state
            at = tile(out, c, head)
            value = at[...] + factor * nn(tile(q, c, head)[...], state)
            at[...] = value
            squares = squares + value * value
            inner = inner + tile(g, c, head)[...].astype(F32) * value
        parts = jnp.concatenate(split(squares) + split(inner), axis=1)
        norm[c] = nt(picks, parts)
        for step in range(1, zs):
            norm_copy(c, step).start()
        return 0

    lax.fori_loop(0, chunks, outputs, 0)

    def grads(i, _):
        c = chunks - 1 - i
        total = norm[c]
        for step in range(1, zs):
            norm_copy(c, step).wait_recv()
            total = total + norm_in[step - 1, c]
        squares, inner = total[0:1], total[4:5]
        recip = lax.rsqrt(squares / (heads_all * HD) + EPSILON)
        coef = recip * recip * recip * inner / (heads_all * HD)
        both = jnp.concatenate(
            [jnp.broadcast_to(recip, (4, CHUNK)), jnp.broadcast_to(coef, (4, CHUNK))], axis=0
        ).T
        recip, coef = both[:, 0:1], both[:, 4:5]
        for head in range(heads):
            value = tile(out, c, head)[...]
            at = tile(g, c, head)
            tile(res, c, head)[...] = (value * recip).astype(BF16)
            at[...] = (recip * at[...].astype(F32) - coef * value).astype(BF16)
        return 0

    lax.fori_loop(0, chunks, grads, 0)

    def local_backward(low, high):
        def one(head, _):
            for c in range(chunks):
                grad = tile(g, c, head)[...]
                keys = tile(k, c, head)[...]
                scores = masked(nt(grad, tile(v, c, head)[...]))
                tile(qg, c, head)[...] = (nn(scores, keys) + factor * nt(grad, pre_bf[head, c])).astype(BF16)
                tile(kp, c, head)[...] = tn(scores, tile(q, c, head)[...])
                tile(vp, c, head)[...] = tn(w[head, c], grad)
            return 0

        lax.fori_loop(low, high, one, 0)

    def qg_states(part):
        states(q, g, backward, order[part], down)

    qg_states(0)
    backward.pair(0).start()
    qg_states(1)
    qg_states(2)
    backward.pair(1).start()
    backward.add_pair(0)
    qg_states(3)
    backward.add_pair(1)
    local_backward(0, 3)
    backward.add_chips(0)
    backward.add_chips(1)
    local_backward(3, 6)
    backward.hand_over(0)
    backward.hand_over(1)
    local_backward(6, heads)
    backward.arrive(0)
    backward.arrive(1)

    def suffixes(head, _):
        for c in range(chunks):
            sfx[head, c] = (factor * (backward.carry[head] + pre[head, c])).astype(BF16)
        return 0

    lax.fori_loop(0, heads, suffixes, 0)

    forward.drain()
    backward.drain()
    for c in range(chunks):
        for step in range(1, zs):
            norm_copy(c, step).wait_send()


def last_kernel(res, qg, kp, vp, k, v, sfx, res_o, qg_o, kg_o, vg_o, kg, vg, sems):
    rows, width = k.shape
    heads, chunks = width // HD, rows // CHUNK
    whole = [pltpu.make_async_copy(res, res_o, sems.at[0, 0]), pltpu.make_async_copy(qg, qg_o, sems.at[1, 0])]
    for copy in whole:
        copy.start()

    def leave(which, c):
        src, dst = ((kg, kg_o), (vg, vg_o))[which]
        at = pl.ds(pl.multiple_of(c * CHUNK, CHUNK), CHUNK)
        return pltpu.make_async_copy(src.at[at], dst.at[at], sems.at[2 + which, c])

    def one(c, _):
        for head in range(heads):
            state = sfx[head, c]
            tile(kg, c, head)[...] = (tile(kp, c, head)[...] + nt(tile(v, c, head)[...], state)).astype(BF16)
            tile(vg, c, head)[...] = (tile(vp, c, head)[...] + nn(tile(k, c, head)[...], state)).astype(BF16)
        leave(0, c).start()
        leave(1, c).start()
        return 0

    lax.fori_loop(0, chunks, one, 0)
    for copy in whole:
        copy.wait()
    for c in range(chunks):
        leave(0, c).wait()
        leave(1, c).wait()


def on_device(queries, keys, values, out_grad):
    rows, width = queries.shape
    heads, chunks = width // HD, rows // CHUNK
    chips, zs = lax.axis_size("seq") // 2, lax.axis_size("head")
    dma = pltpu.SemaphoreType.DMA
    flat, flat32 = pltpu.VMEM((rows, width), BF16), pltpu.VMEM((rows, width), F32)
    in_hbm = pl.BlockSpec(memory_space=pltpu.HBM)
    in_vmem = pl.BlockSpec(memory_space=pltpu.VMEM)
    pair = rows * heads * HD * HD * 2
    held = pl.pallas_call(
        main_kernel,
        out_shape=(flat, flat, flat32, flat32, flat, flat, pltpu.VMEM((heads, chunks, HD, HD), BF16)),
        in_specs=[in_hbm] * 4,
        out_specs=[in_vmem] * 7,
        scratch_shapes=[
            flat,
            flat,
            pltpu.VMEM((heads, chunks, CHUNK, CHUNK), BF16),
            pltpu.VMEM((heads, chunks, HD, HD), F32),
            pltpu.VMEM((heads, chunks, HD, HD), BF16),
            pltpu.VMEM((chunks, 8, CHUNK), F32),
            pltpu.VMEM((zs - 1, chunks, 8, CHUNK), F32),
            dma((4, 2 * STAGES)),
            dma((zs - 1, chunks)),
            dma((zs - 1, chunks)),
        ]
        + scan_scratch(heads, chips)
        + scan_scratch(heads, chips),
        compiler_params=pltpu.CompilerParams(
            collective_id=0, has_side_effects=True, vmem_limit_bytes=26 * MIB
        ),
        cost_estimate=pl.CostEstimate(flops=10 * pair, bytes_accessed=8 * rows * width, transcendentals=0),
        name="attention",
    )(queries, keys, values, out_grad)
    held = [pltpu.with_memory_space_constraint(x, pltpu.VMEM) for x in held]
    like = jax.ShapeDtypeStruct((rows, width), BF16)
    return pl.pallas_call(
        last_kernel,
        out_shape=(like,) * 4,
        in_specs=[in_vmem] * 7,
        out_specs=[in_hbm] * 4,
        scratch_shapes=[flat, flat, dma((4, chunks))],
        compiler_params=pltpu.CompilerParams(vmem_limit_bytes=12 * MIB),
        cost_estimate=pl.CostEstimate(flops=2 * pair, bytes_accessed=8 * rows * width, transcendentals=0),
        name="suffix_gradients",
    )(*held)


def solution(mesh):
    spec = P("seq", "head")
    return jax.shard_map(on_device, mesh=mesh, in_specs=(spec,) * 4, out_specs=(spec,) * 4, check_vma=False)
```

```python
import functools

import jax
import jax.numpy as jnp
from jax import lax
from jax.experimental import pallas as pl
from jax.experimental.pallas import tpu as pltpu
from jax.sharding import PartitionSpec as P

HD = 128
CHUNK = 256
SUB = 128
STAGES = 2
GROUP_HEADS = 4
COLUMNS = 4
NORM_BLOCKS = 4
EPSILON = 1e-05

MESH = pl.DeviceIdType.MESH
F32 = jnp.float32
BF16 = jnp.bfloat16
MIB = 1 << 20


def nn(a, b):
    return lax.dot_general(a, b, (((1,), (0,)), ((), ())), preferred_element_type=F32)


def nt(a, b):
    return lax.dot_general(a, b, (((1,), (1,)), ((), ())), preferred_element_type=F32)


def tn(a, b):
    return lax.dot_general(a, b, (((0,), (0,)), ((), ())), preferred_element_type=F32)


def tile(ref, chunk, head):
    row, col = chunk * CHUNK, head * HD
    if not isinstance(row, int):
        row = pl.multiple_of(row, CHUNK)
    if not isinstance(col, int):
        col = pl.multiple_of(col, HD)
    return ref.at[pl.ds(row, CHUNK), pl.ds(col, HD)]


class Scan:
    def __init__(self, refs, heads, backward):
        self.tot, self.pin, self.mine, self.got, self.pre, self.back, self.snd, self.carry = refs[:8]
        self.pair_s, self.pair_r, self.gat_s, self.gat_r, self.ret_s, self.ret_r, self.fin_s, self.fin_r = refs[8:]
        self.half = heads // 2
        self.width = self.half // STAGES
        self.backward = backward
        self.chips = lax.axis_size("seq") // 2
        self.columns = min(COLUMNS, self.chips // 2)
        self.lines = self.chips // self.columns
        self.offsets = sorted(
            ((i, j) for i in range(self.lines) for j in range(self.columns) if i or j),
            key=lambda at: -(min(at[0], self.lines - at[0]) + min(at[1], self.columns - at[1])),
        )
        seq = lax.axis_index("seq")
        self.core = seq % 2
        self.chip = seq // 2
        self.partner = self.chip * 2 + 1 - self.core
        self.later = (1 - self.core if backward else self.core).astype(F32)

    def own(self, stage):
        return self.core * self.half + stage * self.width

    def other(self, stage):
        return (1 - self.core) * self.half + stage * self.width

    def copy(self, src, dst, send, recv, seq):
        return pltpu.make_async_remote_copy(
            src_ref=src, dst_ref=dst, send_sem=send, recv_sem=recv, device_id={"seq": seq}, device_id_type=MESH
        )

    def pair(self, stage):
        return self.copy(
            self.tot.at[pl.ds(self.other(stage), self.width)],
            self.pin.at[stage],
            self.pair_s.at[stage],
            self.pair_r.at[stage],
            self.partner,
        )

    def chip_at(self, offset):
        x = (self.chip // self.columns + offset[0]) % self.lines
        return x * self.columns + (self.chip + offset[1]) % self.columns

    def gather(self, stage, offset):
        chip = self.chip_at(offset)
        return self.copy(
            self.mine.at[stage, chip],
            self.got.at[stage, self.chip],
            self.gat_s.at[stage],
            self.gat_r.at[stage],
            chip * 2 + self.core,
        )

    def give(self, stage, offset):
        chip = self.chip_at(offset)
        return self.copy(
            self.pre.at[stage, chip],
            self.back.at[stage, self.chip],
            self.ret_s.at[stage],
            self.ret_r.at[stage],
            chip * 2 + self.core,
        )

    def all_gathered(self, stage):
        at = pl.ds(0, self.chips - 1)
        return self.copy(
            self.mine.at[stage, at], self.got.at[stage, at], self.gat_s.at[stage], self.gat_r.at[stage], self.partner
        )

    def all_given(self, stage):
        at = pl.ds(0, self.chips - 1)
        return self.copy(
            self.pre.at[stage, at], self.back.at[stage, at], self.ret_s.at[stage], self.ret_r.at[stage], self.partner
        )

    def finish(self, stage):
        return self.copy(
            self.snd.at[stage],
            self.carry.at[pl.ds(self.own(stage), self.width)],
            self.fin_s.at[stage],
            self.fin_r.at[stage],
            self.partner,
        )

    def add_pair(self, stage):
        self.pair(stage).wait_recv()
        total = self.tot[pl.ds(self.own(stage), self.width)] + self.pin[stage]
        self.mine[stage] = total.reshape(self.mine.shape[1:])
        for offset in self.offsets:
            self.gather(stage, offset).start()
        self.got[stage, self.chip] = self.mine[stage, self.chip]

    def add_chips(self, stage):
        self.all_gathered(stage).wait_recv()
        order = range(self.chips)
        total = jnp.zeros(self.got.shape[2:], F32)
        for chip in reversed(order) if self.backward else order:
            self.pre[stage, chip] = total
            total = total + self.got[stage, chip]
        for offset in self.offsets:
            self.give(stage, offset).start()
        self.back[stage, self.chip] = self.pre[stage, self.chip]

    def hand_over(self, stage):
        self.all_given(stage).wait_recv()
        before = self.back[stage].reshape((self.width, HD, HD))
        own = pl.ds(self.own(stage), self.width)
        self.snd[stage] = before + (1.0 - self.later) * self.tot[own]
        self.finish(stage).start()
        self.carry[own] = before + self.later * self.pin[stage]

    def arrive(self, stage):
        self.finish(stage).wait_recv()

    def drain(self):
        for stage in range(STAGES):
            self.pair(stage).wait_send()
            self.finish(stage).wait_send()
            self.all_gathered(stage).wait_send()
            self.all_given(stage).wait_send()


def scan_scratch(heads, chips):
    half = heads // 2
    width = half // STAGES
    rows = width * HD // chips
    dma = pltpu.SemaphoreType.DMA
    return [
        pltpu.VMEM((heads, HD, HD), F32),
        pltpu.VMEM((STAGES, width, HD, HD), F32),
        pltpu.VMEM((STAGES, chips, rows, HD), F32),
        pltpu.VMEM((STAGES, chips, rows, HD), F32),
        pltpu.VMEM((STAGES, chips, rows, HD), F32),
        pltpu.VMEM((STAGES, chips, rows, HD), F32),
        pltpu.VMEM((STAGES, width, HD, HD), F32),
        pltpu.VMEM((heads, HD, HD), F32),
        dma((STAGES,)),
        dma((STAGES,)),
        dma((STAGES,)),
        dma((STAGES,)),
        dma((STAGES,)),
        dma((STAGES,)),
        dma((STAGES,)),
        dma((STAGES,)),
    ]


SCAN_REFS = 16


def split(x, count):
    terms = []
    for _ in range(count):
        terms.append(x.astype(BF16))
        x = x - terms[-1].astype(F32)
    return terms


def main_kernel(q_hbm, k_hbm, v_hbm, g_hbm, res, qg, kp, vp, k, v, sfx, *scratch):
    q, g, w, pre, pre_bf, recips, coefs, norm, norm_in, in_sem, norm_s, norm_r = scratch[:12]
    fwd_refs = scratch[12 : 12 + SCAN_REFS]
    bwd_refs = scratch[12 + SCAN_REFS :]
    out = vp
    rows, width = q.shape
    heads, chunks = width // HD, rows // CHUNK
    factor = HD ** (-0.5)
    zs = lax.axis_size("head")
    z = lax.axis_index("head")
    features = heads * zs * HD
    forward = Scan(fwd_refs, heads, False)
    backward = Scan(bwd_refs, heads, True)
    core, chips = forward.core, forward.chips
    per = forward.width

    order = []
    for stage in range(STAGES):
        order.append(forward.other(stage))
    for stage in range(STAGES):
        order.append(forward.own(stage))
    parts = len(order)

    def load(which, part):
        src, dst = ((k_hbm, k), (v_hbm, v), (q_hbm, q), (g_hbm, g))[which]
        cols = pl.ds(pl.multiple_of(order[part] * HD, HD), per * HD)
        return pltpu.make_async_copy(src.at[:, cols], dst.at[:, cols], in_sem.at[which, part])

    def load_start(which):
        for part in range(parts):
            load(which, part).start()

    def load_wait(which):
        for part in range(parts):
            load(which, part).wait()

    for part in range(parts):
        load(0, part).start()
        load(1, part).start()
    barrier = pltpu.get_barrier_semaphore()
    pl.semaphore_signal(barrier, inc=1, device_id={"seq": forward.partner}, device_id_type=MESH)
    for offset in forward.offsets:
        pl.semaphore_signal(
            barrier, inc=1, device_id={"seq": forward.chip_at(offset) * 2 + core}, device_id_type=MESH
        )
    for step in range(1, zs):
        pl.semaphore_signal(barrier, inc=1, device_id={"head": (z + step) % zs}, device_id_type=MESH)

    up, down = list(range(chunks)), list(reversed(range(chunks)))

    def kv(part):
        load(0, part).wait()
        load(1, part).wait()
        for i in range(per):
            head = order[part] + i
            total = jnp.zeros((HD, HD), F32)
            for c in up:
                pre[head, c] = total
                total = total + tn(tile(k, c, head)[...], tile(v, c, head)[...])
            forward.tot[head] = total

    row_at = lax.broadcasted_iota(jnp.int32, (SUB, SUB), 0)
    col_at = lax.broadcasted_iota(jnp.int32, (SUB, SUB), 1)
    causal = row_at >= col_at

    def masked(x):
        lines = []
        blocks = CHUNK // SUB
        for i in range(blocks):
            line = []
            for j in range(blocks):
                block = x[i * SUB : (i + 1) * SUB, j * SUB : (j + 1) * SUB] * factor
                if j > i:
                    line.append(jnp.zeros((SUB, SUB), BF16))
                elif j == i:
                    line.append(jnp.where(causal, block, 0.0).astype(BF16))
                else:
                    line.append(block.astype(BF16))
            lines.append(jnp.concatenate(line, axis=1))
        return jnp.concatenate(lines, axis=0)

    def each(body, group=GROUP_HEADS, first=0, last=None):
        def step(i, _):
            for j in range(group):
                for c in range(chunks):
                    body(i * group + j, c)
            return 0

        lax.fori_loop(first // group, (heads if last is None else last) // group, step, 0)

    def flipped(matrix, right):
        lines = []
        for i in range(CHUNK // SUB):
            at = pl.ds(i * SUB, SUB)
            low = pl.ds(i * SUB, CHUNK - i * SUB)
            lines.append(tn(matrix[low, at], right[low, :]))
        return jnp.concatenate(lines, axis=0)

    def scores_step(head, c):
        w[head, c] = masked(nt(tile(q, c, head)[...], tile(k, c, head)[...]))

    def local_step(head, c):
        state = pre[head, c].astype(BF16)
        tile(out, c, head)[...] = nn(w[head, c], tile(v, c, head)[...]) + factor * nn(tile(q, c, head)[...], state)

    kv(0)
    pl.semaphore_wait(barrier, chips - 1 + zs)
    forward.pair(0).start()
    kv(1)
    forward.pair(1).start()
    load_start(2)
    kv(2)
    forward.add_pair(0)
    kv(3)
    forward.add_pair(1)
    load_start(3)
    load_wait(2)
    each(scores_step)
    each(local_step)
    forward.add_chips(0)
    forward.add_chips(1)
    load_wait(3)
    forward.hand_over(0)
    forward.hand_over(1)

    blocks = rows // SUB

    def at_block(b):
        return pl.ds(pl.multiple_of(b * SUB, SUB), SUB)

    def iotas(shape):
        return lax.broadcasted_iota(jnp.int32, shape, 0), lax.broadcasted_iota(jnp.int32, shape, 1)

    def ones_where(condition):
        return jnp.where(condition, 1.0, 0.0).astype(BF16)

    r, c_ = iotas((2 * NORM_BLOCKS, 4 * HD))
    gather_rows = [
        ones_where(r == j + jnp.where(c_ < 2 * HD, 0, NORM_BLOCKS)) for j in range(NORM_BLOCKS)
    ]
    r, c_ = iotas((6 * NORM_BLOCKS, 2 * HD))
    spread_rows = [
        ones_where((r % NORM_BLOCKS == j) & ((r < 3 * NORM_BLOCKS) == (c_ < HD))) for j in range(NORM_BLOCKS)
    ]

    def norm_copy(i, step):
        return pltpu.make_async_remote_copy(
            src_ref=norm.at[i],
            dst_ref=norm_in.at[step - 1, i],
            send_sem=norm_s.at[step - 1, i],
            recv_sem=norm_r.at[step - 1, i],
            device_id={"head": (z + step) % zs},
            device_id_type=MESH,
        )

    def outputs(stage):
        for i in range(2):
            for j in range(per):
                head = order[stage + STAGES * i] + j
                state = forward.carry[head].astype(BF16)
                for c in up:
                    at = tile(out, c, head)
                    at[...] = at[...] + factor * nn(tile(q, c, head)[...], state)

    def row_sums(i, _):
        total = jnp.zeros((2 * NORM_BLOCKS, SUB), F32)
        for j in range(NORM_BLOCKS):
            at = at_block(i * NORM_BLOCKS + j)
            squares, inner = jnp.zeros((SUB, HD), F32), jnp.zeros((SUB, HD), F32)
            for head in range(heads):
                cols = pl.ds(head * HD, HD)
                value = out[at, cols]
                squares = squares + value * value
                inner = inner + g[at, cols].astype(F32) * value
            total = total + nt(gather_rows[j], jnp.concatenate(split(squares, 2) + split(inner, 2), axis=1))
        norm[i] = total
        for to in range(1, zs):
            norm_copy(i, to).start()
        return 0

    for stage in range(STAGES):
        forward.arrive(stage)
        outputs(stage)
    lax.fori_loop(0, blocks // NORM_BLOCKS, row_sums, 0)

    def prefix_step(head, c):
        pre_bf[head, c] = (forward.carry[head] + pre[head, c]).astype(BF16)

    each(prefix_step)

    for i in range(blocks // NORM_BLOCKS):
        total = norm[i]
        for step in range(1, zs):
            norm_copy(i, step).wait_recv()
            total = total + norm_in[step - 1, i]
        squares, inner = total[:NORM_BLOCKS], total[NORM_BLOCKS:]
        recip = lax.rsqrt(squares / features + EPSILON)
        coef = recip * recip * recip * inner / features
        terms = jnp.concatenate([x.astype(F32) for x in split(recip, 3) + split(coef, 3)], axis=0).astype(BF16)
        for j in range(NORM_BLOCKS):
            at = at_block(i * NORM_BLOCKS + j)
            both = tn(terms, spread_rows[j])
            recips[at] = both[:, :HD]
            coefs[at] = both[:, HD:]

    def grad_step(head, c):
        value, recip = tile(out, c, head)[...], recips[pl.ds(c * CHUNK, CHUNK)]
        at = tile(g, c, head)
        at[...] = (recip * at[...].astype(F32) - coefs[pl.ds(c * CHUNK, CHUNK)] * value).astype(BF16)

    def result_step(head, c):
        tile(res, c, head)[...] = (tile(out, c, head)[...] * recips[pl.ds(c * CHUNK, CHUNK)]).astype(BF16)

    def grads(part):
        for i in range(per):
            total = jnp.zeros((HD, HD), F32)
            for c in down:
                if part < parts:
                    grad_step(order[part] + i, c)
                if part > 0:
                    head = order[part - 1] + i
                    pre[head, c] = total
                    total = total + tn(tile(q, c, head)[...], tile(g, c, head)[...])
            if part > 0:
                backward.tot[order[part - 1] + i] = total

    def v_step(head, c):
        tile(vp, c, head)[...] = flipped(w.at[head, c], tile(g, c, head))

    def dscore_step(head, c):
        w[head, c] = masked(nt(tile(g, c, head)[...], tile(v, c, head)[...]))

    def q_step(head, c):
        tile(qg, c, head)[...] = (
            nn(w[head, c], tile(k, c, head)[...]) + factor * nt(tile(g, c, head)[...], pre_bf[head, c])
        ).astype(BF16)

    def k_step(head, c):
        tile(kp, c, head)[...] = flipped(w.at[head, c], tile(q, c, head))

    grads(0)
    grads(1)
    backward.pair(0).start()
    grads(2)
    backward.pair(1).start()
    grads(3)
    backward.add_pair(0)
    grads(4)
    backward.add_pair(1)
    each(result_step)
    each(v_step)
    each(dscore_step)
    each(k_step)
    backward.add_chips(0)
    backward.add_chips(1)
    each(q_step)
    backward.hand_over(0)
    backward.hand_over(1)
    backward.arrive(0)
    backward.arrive(1)

    def suffix_step(head, c):
        sfx[head, c] = (factor * (backward.carry[head] + pre[head, c])).astype(BF16)

    each(suffix_step)

    forward.drain()
    backward.drain()
    for i in range(blocks // NORM_BLOCKS):
        for step in range(1, zs):
            norm_copy(i, step).wait_send()


def last_kernel(res, qg, kp, vp, k, v, sfx, res_o, qg_o, kg_o, vg_o, kg, vg, sems):
    rows, width = k.shape
    heads, chunks = width // HD, rows // CHUNK
    whole = [pltpu.make_async_copy(res, res_o, sems.at[0, 0]), pltpu.make_async_copy(qg, qg_o, sems.at[1, 0])]
    for copy in whole:
        copy.start()

    def leave(which, c):
        src, dst = ((kg, kg_o), (vg, vg_o))[which]
        at = pl.ds(c * CHUNK, CHUNK)
        return pltpu.make_async_copy(src.at[at], dst.at[at], sems.at[2 + which, c])

    for c in range(chunks):
        for head in range(heads):
            state = sfx[head, c]
            tile(kg, c, head)[...] = (tile(kp, c, head)[...] + nt(tile(v, c, head)[...], state)).astype(BF16)
            tile(vg, c, head)[...] = (tile(vp, c, head)[...] + nn(tile(k, c, head)[...], state)).astype(BF16)
        leave(0, c).start()
        leave(1, c).start()
    for copy in whole:
        copy.wait()
    for c in range(chunks):
        leave(0, c).wait()
        leave(1, c).wait()


def on_device(queries, keys, values, out_grad):
    rows, width = queries.shape
    heads, chunks, sums = width // HD, rows // CHUNK, rows // (SUB * NORM_BLOCKS)
    chips, zs = lax.axis_size("seq") // 2, lax.axis_size("head")
    dma = pltpu.SemaphoreType.DMA
    flat, flat32 = pltpu.VMEM((rows, width), BF16), pltpu.VMEM((rows, width), F32)
    in_hbm = pl.BlockSpec(memory_space=pltpu.HBM)
    in_vmem = pl.BlockSpec(memory_space=pltpu.VMEM)
    pair = rows * heads * HD * HD * 2
    held = pl.pallas_call(
        main_kernel,
        out_shape=(flat, flat, flat32, flat32, flat, flat, pltpu.VMEM((heads, chunks, HD, HD), BF16)),
        in_specs=[in_hbm] * 4,
        out_specs=[in_vmem] * 7,
        scratch_shapes=[
            flat,
            flat,
            pltpu.VMEM((heads, chunks, CHUNK, CHUNK), BF16),
            pltpu.VMEM((heads, chunks, HD, HD), F32),
            pltpu.VMEM((heads, chunks, HD, HD), BF16),
            pltpu.VMEM((rows, HD), F32),
            pltpu.VMEM((rows, HD), F32),
            pltpu.VMEM((sums, 2 * NORM_BLOCKS, SUB), F32),
            pltpu.VMEM((zs - 1, sums, 2 * NORM_BLOCKS, SUB), F32),
            dma((4, 2 * STAGES)),
            dma((zs - 1, sums)),
            dma((zs - 1, sums)),
        ]
        + scan_scratch(heads, chips)
        + scan_scratch(heads, chips),
        compiler_params=pltpu.CompilerParams(
            collective_id=0, has_side_effects=True, vmem_limit_bytes=27 * MIB
        ),
        cost_estimate=pl.CostEstimate(flops=10 * pair, bytes_accessed=8 * rows * width, transcendentals=0),
        name="attention",
    )(queries, keys, values, out_grad)
    held = [pltpu.with_memory_space_constraint(x, pltpu.VMEM) for x in held]
    like = jax.ShapeDtypeStruct((rows, width), BF16)
    return pl.pallas_call(
        last_kernel,
        out_shape=(like,) * 4,
        in_specs=[in_vmem] * 7,
        out_specs=[in_hbm] * 4,
        scratch_shapes=[flat, flat, dma((4, chunks))],
        compiler_params=pltpu.CompilerParams(vmem_limit_bytes=12 * MIB),
        cost_estimate=pl.CostEstimate(flops=2 * pair, bytes_accessed=8 * rows * width, transcendentals=0),
        name="suffix_gradients",
    )(*held)


def solution(mesh):
    spec = P("seq", "head")
    return jax.shard_map(on_device, mesh=mesh, in_specs=(spec,) * 4, out_specs=(spec,) * 4, check_vma=False)
```

```python
import functools

import jax
import jax.numpy as jnp
from jax import lax
from jax.experimental import pallas as pl
from jax.experimental.pallas import tpu as pltpu
from jax.sharding import PartitionSpec as P

HD = 128
CHUNK = 256
SUB = 128
STAGES = 2
GROUP_HEADS = 4
COLUMNS = 4
NORM_BLOCKS = 4
EPSILON = 1e-05

MESH = pl.DeviceIdType.MESH
F32 = jnp.float32
BF16 = jnp.bfloat16
MIB = 1 << 20


def nn(a, b):
    return lax.dot_general(a, b, (((1,), (0,)), ((), ())), preferred_element_type=F32)


def nt(a, b):
    return lax.dot_general(a, b, (((1,), (1,)), ((), ())), preferred_element_type=F32)


def tn(a, b):
    return lax.dot_general(a, b, (((0,), (0,)), ((), ())), preferred_element_type=F32)


def tile(ref, chunk, head):
    row, col = chunk * CHUNK, head * HD
    if not isinstance(row, int):
        row = pl.multiple_of(row, CHUNK)
    if not isinstance(col, int):
        col = pl.multiple_of(col, HD)
    return ref.at[pl.ds(row, CHUNK), pl.ds(col, HD)]


class Scan:
    def __init__(self, refs, heads, backward):
        self.tot, self.pin, self.mine, self.got, self.pre, self.back, self.snd, self.carry = refs[:8]
        self.pair_s, self.pair_r, self.gat_s, self.gat_r, self.ret_s, self.ret_r, self.fin_s, self.fin_r = refs[8:]
        self.half = heads // 2
        self.width = self.half // STAGES
        self.backward = backward
        self.chips = lax.axis_size("seq") // 2
        self.columns = min(COLUMNS, self.chips // 2)
        self.lines = self.chips // self.columns
        self.offsets = sorted(
            ((i, j) for i in range(self.lines) for j in range(self.columns) if i or j),
            key=lambda at: -(min(at[0], self.lines - at[0]) + min(at[1], self.columns - at[1])),
        )
        seq = lax.axis_index("seq")
        self.core = seq % 2
        self.chip = seq // 2
        self.partner = self.chip * 2 + 1 - self.core
        self.later = (1 - self.core if backward else self.core).astype(F32)

    def own(self, stage):
        return self.core * self.half + stage * self.width

    def other(self, stage):
        return (1 - self.core) * self.half + stage * self.width

    def copy(self, src, dst, send, recv, seq):
        return pltpu.make_async_remote_copy(
            src_ref=src, dst_ref=dst, send_sem=send, recv_sem=recv, device_id={"seq": seq}, device_id_type=MESH
        )

    def pair(self, stage):
        return self.copy(
            self.tot.at[pl.ds(self.other(stage), self.width)],
            self.pin.at[stage],
            self.pair_s.at[stage],
            self.pair_r.at[stage],
            self.partner,
        )

    def chip_at(self, offset):
        x = (self.chip // self.columns + offset[0]) % self.lines
        return x * self.columns + (self.chip + offset[1]) % self.columns

    def gather(self, stage, offset):
        chip = self.chip_at(offset)
        return self.copy(
            self.mine.at[stage, chip],
            self.got.at[stage, self.chip],
            self.gat_s.at[stage],
            self.gat_r.at[stage],
            chip * 2 + self.core,
        )

    def give(self, stage, offset):
        chip = self.chip_at(offset)
        return self.copy(
            self.pre.at[stage, chip],
            self.back.at[stage, self.chip],
            self.ret_s.at[stage],
            self.ret_r.at[stage],
            chip * 2 + self.core,
        )

    def all_gathered(self, stage):
        at = pl.ds(0, self.chips - 1)
        return self.copy(
            self.mine.at[stage, at], self.got.at[stage, at], self.gat_s.at[stage], self.gat_r.at[stage], self.partner
        )

    def all_given(self, stage):
        at = pl.ds(0, self.chips - 1)
        return self.copy(
            self.pre.at[stage, at], self.back.at[stage, at], self.ret_s.at[stage], self.ret_r.at[stage], self.partner
        )

    def finish(self, stage):
        return self.copy(
            self.snd.at[stage],
            self.carry.at[pl.ds(self.own(stage), self.width)],
            self.fin_s.at[stage],
            self.fin_r.at[stage],
            self.partner,
        )

    def add_pair(self, stage):
        self.pair(stage).wait_recv()
        total = self.tot[pl.ds(self.own(stage), self.width)] + self.pin[stage]
        self.mine[stage] = total.reshape(self.mine.shape[1:])
        for offset in self.offsets:
            self.gather(stage, offset).start()
        self.got[stage, self.chip] = self.mine[stage, self.chip]

    def add_chips(self, stage):
        self.all_gathered(stage).wait_recv()
        order = range(self.chips)
        total = jnp.zeros(self.got.shape[2:], F32)
        for chip in reversed(order) if self.backward else order:
            self.pre[stage, chip] = total
            total = total + self.got[stage, chip]
        for offset in self.offsets:
            self.give(stage, offset).start()
        self.back[stage, self.chip] = self.pre[stage, self.chip]

    def hand_over(self, stage):
        self.all_given(stage).wait_recv()
        before = self.back[stage].reshape((self.width, HD, HD))
        own = pl.ds(self.own(stage), self.width)
        self.snd[stage] = before + (1.0 - self.later) * self.tot[own]
        self.finish(stage).start()
        self.carry[own] = before + self.later * self.pin[stage]

    def arrive(self, stage):
        self.finish(stage).wait_recv()

    def drain(self):
        for stage in range(STAGES):
            self.pair(stage).wait_send()
            self.finish(stage).wait_send()
            self.all_gathered(stage).wait_send()
            self.all_given(stage).wait_send()


def scan_scratch(heads, chips):
    half = heads // 2
    width = half // STAGES
    rows = width * HD // chips
    dma = pltpu.SemaphoreType.DMA
    return [
        pltpu.VMEM((heads, HD, HD), F32),
        pltpu.VMEM((STAGES, width, HD, HD), F32),
        pltpu.VMEM((STAGES, chips, rows, HD), F32),
        pltpu.VMEM((STAGES, chips, rows, HD), F32),
        pltpu.VMEM((STAGES, chips, rows, HD), F32),
        pltpu.VMEM((STAGES, chips, rows, HD), F32),
        pltpu.VMEM((STAGES, width, HD, HD), F32),
        pltpu.VMEM((heads, HD, HD), F32),
        dma((STAGES,)),
        dma((STAGES,)),
        dma((STAGES,)),
        dma((STAGES,)),
        dma((STAGES,)),
        dma((STAGES,)),
        dma((STAGES,)),
        dma((STAGES,)),
    ]


SCAN_REFS = 16


def split(x, count):
    terms = []
    for _ in range(count):
        terms.append(x.astype(BF16))
        x = x - terms[-1].astype(F32)
    return terms


def main_kernel(q_hbm, k_hbm, v_hbm, g_hbm, res, qg, kp, vp, k, v, sfx, *scratch):
    q, g, w, pre, pre_bf, recips, coefs, norm, norm_in, in_sem, norm_s, norm_r = scratch[:12]
    fwd_refs = scratch[12 : 12 + SCAN_REFS]
    bwd_refs = scratch[12 + SCAN_REFS :]
    out = vp
    near = kp
    given = qg
    rows, width = q.shape
    heads, chunks = width // HD, rows // CHUNK
    factor = HD ** (-0.5)
    zs = lax.axis_size("head")
    z = lax.axis_index("head")
    features = heads * zs * HD
    forward = Scan(fwd_refs, heads, False)
    backward = Scan(bwd_refs, heads, True)
    core, chips = forward.core, forward.chips
    per = forward.width

    order = []
    for stage in range(STAGES):
        order.append(forward.other(stage))
    for stage in range(STAGES):
        order.append(forward.own(stage))
    parts = len(order)

    def load(which, part):
        src, dst = ((k_hbm, k), (v_hbm, v), (q_hbm, q), (g_hbm, given))[which]
        cols = pl.ds(pl.multiple_of(order[part] * HD, HD), per * HD)
        return pltpu.make_async_copy(src.at[:, cols], dst.at[:, cols], in_sem.at[which, part])

    def load_start(which):
        for part in range(parts):
            load(which, part).start()

    def load_wait(which):
        for part in range(parts):
            load(which, part).wait()

    for part in range(parts):
        load(0, part).start()
        load(1, part).start()
    barrier = pltpu.get_barrier_semaphore()
    pl.semaphore_signal(barrier, inc=1, device_id={"seq": forward.partner}, device_id_type=MESH)
    for offset in forward.offsets:
        pl.semaphore_signal(
            barrier, inc=1, device_id={"seq": forward.chip_at(offset) * 2 + core}, device_id_type=MESH
        )
    for step in range(1, zs):
        pl.semaphore_signal(barrier, inc=1, device_id={"head": (z + step) % zs}, device_id_type=MESH)

    up, down = list(range(chunks)), list(reversed(range(chunks)))

    def kv(part):
        load(0, part).wait()
        load(1, part).wait()
        for i in range(per):
            head = order[part] + i
            total = jnp.zeros((HD, HD), F32)
            for c in up:
                pre[head, c] = total
                total = total + tn(tile(k, c, head)[...], tile(v, c, head)[...])
            forward.tot[head] = total

    row_at = lax.broadcasted_iota(jnp.int32, (SUB, SUB), 0)
    col_at = lax.broadcasted_iota(jnp.int32, (SUB, SUB), 1)
    causal = row_at >= col_at

    def masked(x):
        lines = []
        blocks = CHUNK // SUB
        for i in range(blocks):
            line = []
            for j in range(blocks):
                block = x[i * SUB : (i + 1) * SUB, j * SUB : (j + 1) * SUB] * factor
                if j > i:
                    line.append(jnp.zeros((SUB, SUB), BF16))
                elif j == i:
                    line.append(jnp.where(causal, block, 0.0).astype(BF16))
                else:
                    line.append(block.astype(BF16))
            lines.append(jnp.concatenate(line, axis=1))
        return jnp.concatenate(lines, axis=0)

    def each(body, group=GROUP_HEADS, first=0, last=None):
        def step(i, _):
            for j in range(group):
                for c in range(chunks):
                    body(i * group + j, c)
            return 0

        lax.fori_loop(first // group, (heads if last is None else last) // group, step, 0)

    def flipped(matrix, right):
        lines = []
        for i in range(CHUNK // SUB):
            at = pl.ds(i * SUB, SUB)
            low = pl.ds(i * SUB, CHUNK - i * SUB)
            lines.append(tn(matrix[low, at], right[low, :]))
        return jnp.concatenate(lines, axis=0)

    def scores_step(head, c):
        w[head, c] = masked(nt(tile(q, c, head)[...], tile(k, c, head)[...]))

    def local_step(head, c):
        state = pre[head, c].astype(BF16)
        tile(near, c, head)[...] = nn(w[head, c], tile(v, c, head)[...]) + factor * nn(tile(q, c, head)[...], state)

    kv(0)
    pl.semaphore_wait(barrier, chips - 1 + zs)
    forward.pair(0).start()
    kv(1)
    forward.pair(1).start()
    load_start(2)
    kv(2)
    forward.add_pair(0)
    kv(3)
    forward.add_pair(1)
    load_start(3)
    load_wait(2)
    each(scores_step)
    each(local_step, last=heads // 2)
    forward.add_chips(0)
    forward.add_chips(1)
    each(local_step, first=heads // 2)
    load_wait(3)

    blocks = rows // SUB

    def at_block(b):
        return pl.ds(pl.multiple_of(b * SUB, SUB), SUB)

    def iotas(shape):
        return lax.broadcasted_iota(jnp.int32, shape, 0), lax.broadcasted_iota(jnp.int32, shape, 1)

    def ones_where(condition):
        return jnp.where(condition, 1.0, 0.0).astype(BF16)

    r, c_ = iotas((2 * NORM_BLOCKS, 4 * HD))
    gather_rows = [
        ones_where(r == j + jnp.where(c_ < 2 * HD, 0, NORM_BLOCKS)) for j in range(NORM_BLOCKS)
    ]
    r, c_ = iotas((6 * NORM_BLOCKS, 2 * HD))
    spread_rows = [
        ones_where((r % NORM_BLOCKS == j) & ((r < 3 * NORM_BLOCKS) == (c_ < HD))) for j in range(NORM_BLOCKS)
    ]

    def norm_copy(i, step):
        return pltpu.make_async_remote_copy(
            src_ref=norm.at[i],
            dst_ref=norm_in.at[step - 1, i],
            send_sem=norm_s.at[step - 1, i],
            recv_sem=norm_r.at[step - 1, i],
            device_id={"head": (z + step) % zs},
            device_id_type=MESH,
        )

    def outputs(part):
        for i in range(per):
            head = order[part] + i
            state = forward.carry[head].astype(BF16)
            for c in up:
                tile(out, c, head)[...] = tile(near, c, head)[...] + factor * nn(tile(q, c, head)[...], state)

    def row_sums(i, _):
        total = jnp.zeros((2 * NORM_BLOCKS, SUB), F32)
        for j in range(NORM_BLOCKS):
            at = at_block(i * NORM_BLOCKS + j)
            squares, inner = jnp.zeros((SUB, HD), F32), jnp.zeros((SUB, HD), F32)
            for head in range(heads):
                cols = pl.ds(head * HD, HD)
                value = out[at, cols]
                squares = squares + value * value
                inner = inner + given[at, cols].astype(F32) * value
            total = total + nt(gather_rows[j], jnp.concatenate(split(squares, 2) + split(inner, 2), axis=1))
        norm[i] = total
        for to in range(1, zs):
            norm_copy(i, to).start()
        return 0

    for stage in range(STAGES):
        forward.hand_over(stage)
        outputs(STAGES + stage)
    for stage in range(STAGES):
        forward.arrive(stage)
        outputs(stage)
    lax.fori_loop(0, blocks // NORM_BLOCKS, row_sums, 0)

    def prefix_step(head, c):
        pre_bf[head, c] = (forward.carry[head] + pre[head, c]).astype(BF16)

    each(prefix_step)

    for i in range(blocks // NORM_BLOCKS):
        total = norm[i]
        for step in range(1, zs):
            norm_copy(i, step).wait_recv()
            total = total + norm_in[step - 1, i]
        squares, inner = total[:NORM_BLOCKS], total[NORM_BLOCKS:]
        recip = lax.rsqrt(squares / features + EPSILON)
        coef = recip * recip * recip * inner / features
        terms = jnp.concatenate([x.astype(F32) for x in split(recip, 3) + split(coef, 3)], axis=0).astype(BF16)
        for j in range(NORM_BLOCKS):
            at = at_block(i * NORM_BLOCKS + j)
            both = tn(terms, spread_rows[j])
            recips[at] = both[:, :HD]
            coefs[at] = both[:, HD:]

    def grad_step(head, c):
        value, recip = tile(out, c, head)[...], recips[pl.ds(c * CHUNK, CHUNK)]
        grad = recip * tile(given, c, head)[...].astype(F32) - coefs[pl.ds(c * CHUNK, CHUNK)] * value
        tile(g, c, head)[...] = grad.astype(BF16)

    def result_step(head, c):
        tile(res, c, head)[...] = (tile(out, c, head)[...] * recips[pl.ds(c * CHUNK, CHUNK)]).astype(BF16)

    def grads(part):
        for i in range(per):
            total = jnp.zeros((HD, HD), F32)
            for c in down:
                if part < parts:
                    grad_step(order[part] + i, c)
                if part > 0:
                    head = order[part - 1] + i
                    pre[head, c] = total
                    total = total + tn(tile(q, c, head)[...], tile(g, c, head)[...])
            if part > 0:
                backward.tot[order[part - 1] + i] = total

    def v_step(head, c):
        tile(vp, c, head)[...] = flipped(w.at[head, c], tile(g, c, head))

    def dscore_step(head, c):
        w[head, c] = masked(nt(tile(g, c, head)[...], tile(v, c, head)[...]))

    def q_step(head, c):
        tile(qg, c, head)[...] = (
            nn(w[head, c], tile(k, c, head)[...]) + factor * nt(tile(g, c, head)[...], pre_bf[head, c])
        ).astype(BF16)

    def k_step(head, c):
        tile(kp, c, head)[...] = flipped(w.at[head, c], tile(q, c, head))

    grads(0)
    grads(1)
    backward.pair(0).start()
    grads(2)
    backward.pair(1).start()
    grads(3)
    backward.add_pair(0)
    grads(4)
    backward.add_pair(1)
    each(result_step)
    each(v_step)
    each(dscore_step)
    backward.add_chips(0)
    backward.add_chips(1)
    each(k_step)
    each(q_step)
    forward.drain()
    for i in range(blocks // NORM_BLOCKS):
        for step in range(1, zs):
            norm_copy(i, step).wait_send()

    def suffixes(part):
        for i in range(per):
            head = order[part] + i
            state = backward.carry[head]
            for c in up:
                sfx[head, c] = (factor * (state + pre[head, c])).astype(BF16)

    for stage in range(STAGES):
        backward.hand_over(stage)
        suffixes(STAGES + stage)
    for stage in range(STAGES):
        backward.arrive(stage)
        suffixes(stage)
    backward.drain()


def last_kernel(res, qg, kp, vp, k, v, sfx, res_o, qg_o, kg_o, vg_o, kg, vg, sems):
    rows, width = k.shape
    heads, chunks = width // HD, rows // CHUNK
    whole = [pltpu.make_async_copy(res, res_o, sems.at[0, 0]), pltpu.make_async_copy(qg, qg_o, sems.at[1, 0])]
    for copy in whole:
        copy.start()

    def leave(which, c):
        src, dst = ((kg, kg_o), (vg, vg_o))[which]
        at = pl.ds(c * CHUNK, CHUNK)
        return pltpu.make_async_copy(src.at[at], dst.at[at], sems.at[2 + which, c])

    for c in range(chunks):
        for head in range(heads):
            state = sfx[head, c]
            tile(kg, c, head)[...] = (tile(kp, c, head)[...] + nt(tile(v, c, head)[...], state)).astype(BF16)
            tile(vg, c, head)[...] = (tile(vp, c, head)[...] + nn(tile(k, c, head)[...], state)).astype(BF16)
        leave(0, c).start()
        leave(1, c).start()
    for copy in whole:
        copy.wait()
    for c in range(chunks):
        leave(0, c).wait()
        leave(1, c).wait()


def on_device(queries, keys, values, out_grad):
    rows, width = queries.shape
    heads, chunks, sums = width // HD, rows // CHUNK, rows // (SUB * NORM_BLOCKS)
    chips, zs = lax.axis_size("seq") // 2, lax.axis_size("head")
    dma = pltpu.SemaphoreType.DMA
    flat, flat32 = pltpu.VMEM((rows, width), BF16), pltpu.VMEM((rows, width), F32)
    in_hbm = pl.BlockSpec(memory_space=pltpu.HBM)
    in_vmem = pl.BlockSpec(memory_space=pltpu.VMEM)
    pair = rows * heads * HD * HD * 2
    held = pl.pallas_call(
        main_kernel,
        out_shape=(flat, flat, flat32, flat32, flat, flat, pltpu.VMEM((heads, chunks, HD, HD), BF16)),
        in_specs=[in_hbm] * 4,
        out_specs=[in_vmem] * 7,
        scratch_shapes=[
            flat,
            flat,
            pltpu.VMEM((heads, chunks, CHUNK, CHUNK), BF16),
            pltpu.VMEM((heads, chunks, HD, HD), F32),
            pltpu.VMEM((heads, chunks, HD, HD), BF16),
            pltpu.VMEM((rows, HD), F32),
            pltpu.VMEM((rows, HD), F32),
            pltpu.VMEM((sums, 2 * NORM_BLOCKS, SUB), F32),
            pltpu.VMEM((zs - 1, sums, 2 * NORM_BLOCKS, SUB), F32),
            dma((4, 2 * STAGES)),
            dma((zs - 1, sums)),
            dma((zs - 1, sums)),
        ]
        + scan_scratch(heads, chips)
        + scan_scratch(heads, chips),
        compiler_params=pltpu.CompilerParams(
            collective_id=0, has_side_effects=True, vmem_limit_bytes=27 * MIB
        ),
        cost_estimate=pl.CostEstimate(flops=10 * pair, bytes_accessed=8 * rows * width, transcendentals=0),
        name="attention",
    )(queries, keys, values, out_grad)
    held = [pltpu.with_memory_space_constraint(x, pltpu.VMEM) for x in held]
    like = jax.ShapeDtypeStruct((rows, width), BF16)
    return pl.pallas_call(
        last_kernel,
        out_shape=(like,) * 4,
        in_specs=[in_vmem] * 7,
        out_specs=[in_hbm] * 4,
        scratch_shapes=[flat, flat, dma((4, chunks))],
        compiler_params=pltpu.CompilerParams(vmem_limit_bytes=12 * MIB),
        cost_estimate=pl.CostEstimate(flops=2 * pair, bytes_accessed=8 * rows * width, transcendentals=0),
        name="suffix_gradients",
    )(*held)


def solution(mesh):
    spec = P("seq", "head")
    return jax.shard_map(on_device, mesh=mesh, in_specs=(spec,) * 4, out_specs=(spec,) * 4, check_vma=False)
```

```python
import functools

import jax
import jax.numpy as jnp
from jax import lax
from jax.experimental import pallas as pl
from jax.experimental.pallas import tpu as pltpu
from jax.sharding import PartitionSpec as P

HD = 128
CHUNK = 256
SUB = 128
STAGES = 2
GROUP_HEADS = 4
COLUMNS = 4
NORM_BLOCKS = 4
EPSILON = 1e-05

MESH = pl.DeviceIdType.MESH
F32 = jnp.float32
BF16 = jnp.bfloat16
MIB = 1 << 20


def nn(a, b):
    return lax.dot_general(a, b, (((1,), (0,)), ((), ())), preferred_element_type=F32)


def nt(a, b):
    return lax.dot_general(a, b, (((1,), (1,)), ((), ())), preferred_element_type=F32)


def tn(a, b):
    return lax.dot_general(a, b, (((0,), (0,)), ((), ())), preferred_element_type=F32)


def tile(ref, chunk, head):
    row, col = chunk * CHUNK, head * HD
    if not isinstance(row, int):
        row = pl.multiple_of(row, CHUNK)
    if not isinstance(col, int):
        col = pl.multiple_of(col, HD)
    return ref.at[pl.ds(row, CHUNK), pl.ds(col, HD)]


class Scan:
    def __init__(self, refs, heads, backward):
        self.tot, self.pin, self.mine, self.got, self.pre, self.back, self.snd, self.carry = refs[:8]
        self.pair_s, self.pair_r, self.gat_s, self.gat_r, self.ret_s, self.ret_r, self.fin_s, self.fin_r = refs[8:]
        self.half = heads // 2
        self.width = self.half // STAGES
        self.backward = backward
        self.chips = lax.axis_size("seq") // 2
        self.columns = min(COLUMNS, self.chips // 2)
        self.lines = self.chips // self.columns
        self.offsets = sorted(
            ((i, j) for i in range(self.lines) for j in range(self.columns) if i or j),
            key=lambda at: -(min(at[0], self.lines - at[0]) + min(at[1], self.columns - at[1])),
        )
        seq = lax.axis_index("seq")
        self.core = seq % 2
        self.chip = seq // 2
        self.partner = self.chip * 2 + 1 - self.core
        self.later = (1 - self.core if backward else self.core).astype(F32)

    def own(self, stage):
        return self.core * self.half + stage * self.width

    def other(self, stage):
        return (1 - self.core) * self.half + stage * self.width

    def copy(self, src, dst, send, recv, seq):
        return pltpu.make_async_remote_copy(
            src_ref=src, dst_ref=dst, send_sem=send, recv_sem=recv, device_id={"seq": seq}, device_id_type=MESH
        )

    def pair(self, stage):
        return self.copy(
            self.tot.at[pl.ds(self.other(stage), self.width)],
            self.pin.at[stage],
            self.pair_s.at[stage],
            self.pair_r.at[stage],
            self.partner,
        )

    def chip_at(self, offset):
        x = (self.chip // self.columns + offset[0]) % self.lines
        return x * self.columns + (self.chip + offset[1]) % self.columns

    def gather(self, stage, offset):
        chip = self.chip_at(offset)
        return self.copy(
            self.mine.at[stage, chip],
            self.got.at[stage, self.chip],
            self.gat_s.at[stage],
            self.gat_r.at[stage],
            chip * 2 + self.core,
        )

    def give(self, stage, offset):
        chip = self.chip_at(offset)
        return self.copy(
            self.pre.at[stage, chip],
            self.back.at[stage, self.chip],
            self.ret_s.at[stage],
            self.ret_r.at[stage],
            chip * 2 + self.core,
        )

    def all_gathered(self, stage):
        at = pl.ds(0, self.chips - 1)
        return self.copy(
            self.mine.at[stage, at], self.got.at[stage, at], self.gat_s.at[stage], self.gat_r.at[stage], self.partner
        )

    def all_given(self, stage):
        at = pl.ds(0, self.chips - 1)
        return self.copy(
            self.pre.at[stage, at], self.back.at[stage, at], self.ret_s.at[stage], self.ret_r.at[stage], self.partner
        )

    def finish(self, stage):
        return self.copy(
            self.snd.at[stage],
            self.carry.at[pl.ds(self.own(stage), self.width)],
            self.fin_s.at[stage],
            self.fin_r.at[stage],
            self.partner,
        )

    def add_pair(self, stage):
        self.pair(stage).wait_recv()
        total = self.tot[pl.ds(self.own(stage), self.width)] + self.pin[stage]
        self.mine[stage] = total.reshape(self.mine.shape[1:])
        for offset in self.offsets:
            self.gather(stage, offset).start()
        self.got[stage, self.chip] = self.mine[stage, self.chip]

    def add_chips(self, stage):
        self.all_gathered(stage).wait_recv()
        order = range(self.chips)
        total = jnp.zeros(self.got.shape[2:], F32)
        for chip in reversed(order) if self.backward else order:
            self.pre[stage, chip] = total
            total = total + self.got[stage, chip]
        for offset in self.offsets:
            self.give(stage, offset).start()
        self.back[stage, self.chip] = self.pre[stage, self.chip]

    def hand_over(self, stage):
        self.all_given(stage).wait_recv()
        before = self.back[stage].reshape((self.width, HD, HD))
        own = pl.ds(self.own(stage), self.width)
        self.snd[stage] = before + (1.0 - self.later) * self.tot[own]
        self.finish(stage).start()
        self.carry[own] = before + self.later * self.pin[stage]

    def arrive(self, stage):
        self.finish(stage).wait_recv()

    def drain(self):
        for stage in range(STAGES):
            self.pair(stage).wait_send()
            self.finish(stage).wait_send()
            self.all_gathered(stage).wait_send()
            self.all_given(stage).wait_send()


def scan_scratch(heads, chips):
    half = heads // 2
    width = half // STAGES
    rows = width * HD // chips
    dma = pltpu.SemaphoreType.DMA
    return [
        pltpu.VMEM((heads, HD, HD), F32),
        pltpu.VMEM((STAGES, width, HD, HD), F32),
        pltpu.VMEM((STAGES, chips, rows, HD), F32),
        pltpu.VMEM((STAGES, chips, rows, HD), F32),
        pltpu.VMEM((STAGES, chips, rows, HD), F32),
        pltpu.VMEM((STAGES, chips, rows, HD), F32),
        pltpu.VMEM((STAGES, width, HD, HD), F32),
        pltpu.VMEM((heads, HD, HD), F32),
        dma((STAGES,)),
        dma((STAGES,)),
        dma((STAGES,)),
        dma((STAGES,)),
        dma((STAGES,)),
        dma((STAGES,)),
        dma((STAGES,)),
        dma((STAGES,)),
    ]


SCAN_REFS = 16


def split(x, count):
    terms = []
    for _ in range(count):
        terms.append(x.astype(BF16))
        x = x - terms[-1].astype(F32)
    return terms


def main_kernel(q_hbm, k_hbm, v_hbm, g_hbm, res, qg, kp, vp, k, v, sfx, *scratch):
    q, g, w, pre, pre_bf, recips, coefs, norm, norm_in, in_sem, norm_s, norm_r = scratch[:12]
    fwd_refs = scratch[12 : 12 + SCAN_REFS]
    bwd_refs = scratch[12 + SCAN_REFS :]
    out = vp
    near = kp
    given = qg
    rows, width = q.shape
    heads, chunks = width // HD, rows // CHUNK
    factor = HD ** (-0.5)
    zs = lax.axis_size("head")
    z = lax.axis_index("head")
    features = heads * zs * HD
    forward = Scan(fwd_refs, heads, False)
    backward = Scan(bwd_refs, heads, True)
    core, chips = forward.core, forward.chips
    per = forward.width

    order = []
    for stage in range(STAGES):
        order.append(forward.other(stage))
    for stage in range(STAGES):
        order.append(forward.own(stage))
    parts = len(order)

    def load(which, part):
        src, dst = ((k_hbm, k), (v_hbm, v), (q_hbm, q), (g_hbm, given))[which]
        cols = pl.ds(pl.multiple_of(order[part] * HD, HD), per * HD)
        return pltpu.make_async_copy(src.at[:, cols], dst.at[:, cols], in_sem.at[which, part])

    def load_start(which):
        for part in range(parts):
            load(which, part).start()

    def load_wait(which):
        for part in range(parts):
            load(which, part).wait()

    for part in range(parts):
        load(0, part).start()
        load(1, part).start()
    barrier = pltpu.get_barrier_semaphore()
    pl.semaphore_signal(barrier, inc=1, device_id={"seq": forward.partner}, device_id_type=MESH)
    for offset in forward.offsets:
        pl.semaphore_signal(
            barrier, inc=1, device_id={"seq": forward.chip_at(offset) * 2 + core}, device_id_type=MESH
        )
    for step in range(1, zs):
        pl.semaphore_signal(barrier, inc=1, device_id={"head": (z + step) % zs}, device_id_type=MESH)

    up, down = list(range(chunks)), list(reversed(range(chunks)))

    def kv(part):
        load(0, part).wait()
        load(1, part).wait()
        for i in range(per):
            head = order[part] + i
            total = jnp.zeros((HD, HD), F32)
            for c in up:
                pre[head, c] = total
                total = total + tn(tile(k, c, head)[...], tile(v, c, head)[...])
            forward.tot[head] = total

    row_at = lax.broadcasted_iota(jnp.int32, (SUB, SUB), 0)
    col_at = lax.broadcasted_iota(jnp.int32, (SUB, SUB), 1)
    causal = row_at >= col_at

    def masked(x):
        lines = []
        blocks = CHUNK // SUB
        for i in range(blocks):
            line = []
            for j in range(blocks):
                block = x[i * SUB : (i + 1) * SUB, j * SUB : (j + 1) * SUB] * factor
                if j > i:
                    line.append(jnp.zeros((SUB, SUB), BF16))
                elif j == i:
                    line.append(jnp.where(causal, block, 0.0).astype(BF16))
                else:
                    line.append(block.astype(BF16))
            lines.append(jnp.concatenate(line, axis=1))
        return jnp.concatenate(lines, axis=0)

    def each(body, group=GROUP_HEADS, first=0, last=None):
        def step(i, _):
            for j in range(group):
                for c in range(chunks):
                    body(i * group + j, c)
            return 0

        lax.fori_loop(first // group, (heads if last is None else last) // group, step, 0)

    def flipped(matrix, right):
        lines = []
        for i in range(CHUNK // SUB):
            at = pl.ds(i * SUB, SUB)
            low = pl.ds(i * SUB, CHUNK - i * SUB)
            lines.append(tn(matrix[low, at], right[low, :]))
        return jnp.concatenate(lines, axis=0)

    def scores_step(head, c):
        w[head, c] = masked(nt(tile(q, c, head)[...], tile(k, c, head)[...]))

    def local_step(head, c):
        state = pre[head, c].astype(BF16)
        tile(near, c, head)[...] = nn(w[head, c], tile(v, c, head)[...]) + factor * nn(tile(q, c, head)[...], state)

    for stage in range(STAGES):
        kv(stage)
        if stage == 0:
            pl.semaphore_wait(barrier, chips - 1 + zs)
        forward.pair(stage).start()
    load_start(2)
    for stage in range(STAGES):
        kv(STAGES + stage)
        forward.add_pair(stage)
    load_start(3)
    load_wait(2)
    each(scores_step)
    each(local_step, last=heads // 2)
    for stage in range(STAGES):
        forward.add_chips(stage)
    each(local_step, first=heads // 2)
    load_wait(3)

    blocks = rows // SUB

    def at_block(b):
        return pl.ds(b * SUB, SUB)

    def iotas(shape):
        return lax.broadcasted_iota(jnp.int32, shape, 0), lax.broadcasted_iota(jnp.int32, shape, 1)

    def ones_where(condition):
        return jnp.where(condition, 1.0, 0.0).astype(BF16)

    r, c_ = iotas((2 * NORM_BLOCKS, 4 * HD))
    gather_rows = [
        ones_where(r == j + jnp.where(c_ < 2 * HD, 0, NORM_BLOCKS)) for j in range(NORM_BLOCKS)
    ]
    r, c_ = iotas((6 * NORM_BLOCKS, 2 * HD))
    spread_rows = [
        ones_where((r % NORM_BLOCKS == j) & ((r < 3 * NORM_BLOCKS) == (c_ < HD))) for j in range(NORM_BLOCKS)
    ]

    def norm_copy(i, step):
        return pltpu.make_async_remote_copy(
            src_ref=norm.at[i],
            dst_ref=norm_in.at[step - 1, i],
            send_sem=norm_s.at[step - 1, i],
            recv_sem=norm_r.at[step - 1, i],
            device_id={"head": (z + step) % zs},
            device_id_type=MESH,
        )

    def outputs(part):
        for i in range(per):
            head = order[part] + i
            state = forward.carry[head].astype(BF16)
            for c in up:
                tile(out, c, head)[...] = tile(near, c, head)[...] + factor * nn(tile(q, c, head)[...], state)

    def row_sums(i):
        total = jnp.zeros((2 * NORM_BLOCKS, SUB), F32)
        for j in range(NORM_BLOCKS):
            at = at_block(i * NORM_BLOCKS + j)
            squares, inner = jnp.zeros((SUB, HD), F32), jnp.zeros((SUB, HD), F32)
            for head in range(heads):
                cols = pl.ds(head * HD, HD)
                value = out[at, cols]
                squares = squares + value * value
                inner = inner + given[at, cols].astype(F32) * value
            total = total + nt(gather_rows[j], jnp.concatenate(split(squares, 2) + split(inner, 2), axis=1))
        norm[i] = total
        for to in sorted(range(1, zs), key=lambda to: -min(to, zs - to)):
            norm_copy(i, to).start()

    for stage in range(STAGES):
        forward.hand_over(stage)
        outputs(STAGES + stage)
    for stage in range(STAGES):
        forward.arrive(stage)
        outputs(stage)
    for i in range(blocks // NORM_BLOCKS):
        row_sums(i)

    def prefix_step(head, c):
        pre_bf[head, c] = (forward.carry[head] + pre[head, c]).astype(BF16)

    each(prefix_step)

    for i in range(blocks // NORM_BLOCKS):
        total = norm[i]
        for step in range(1, zs):
            norm_copy(i, step).wait_recv()
            total = total + norm_in[step - 1, i]
        squares, inner = total[:NORM_BLOCKS], total[NORM_BLOCKS:]
        recip = lax.rsqrt(squares / features + EPSILON)
        coef = recip * recip * recip * inner / features
        terms = jnp.concatenate([x.astype(F32) for x in split(recip, 3) + split(coef, 3)], axis=0).astype(BF16)
        for j in range(NORM_BLOCKS):
            at = at_block(i * NORM_BLOCKS + j)
            both = tn(terms, spread_rows[j])
            recips[at] = both[:, :HD]
            coefs[at] = both[:, HD:]

    def grad_step(head, c):
        value, recip = tile(out, c, head)[...], recips[pl.ds(c * CHUNK, CHUNK)]
        grad = recip * tile(given, c, head)[...].astype(F32) - coefs[pl.ds(c * CHUNK, CHUNK)] * value
        tile(g, c, head)[...] = grad.astype(BF16)

    def result_step(head, c):
        tile(res, c, head)[...] = (tile(out, c, head)[...] * recips[pl.ds(c * CHUNK, CHUNK)]).astype(BF16)

    def grads(part):
        for i in range(per):
            total = jnp.zeros((HD, HD), F32)
            for c in down:
                if part < parts:
                    grad_step(order[part] + i, c)
                if part > 0:
                    head = order[part - 1] + i
                    pre[head, c] = total
                    total = total + tn(tile(q, c, head)[...], tile(g, c, head)[...])
            if part > 0:
                backward.tot[order[part - 1] + i] = total

    def v_step(head, c):
        tile(vp, c, head)[...] = flipped(w.at[head, c], tile(g, c, head))

    def dscore_step(head, c):
        w[head, c] = masked(nt(tile(g, c, head)[...], tile(v, c, head)[...]))

    def q_step(head, c):
        tile(qg, c, head)[...] = (
            nn(w[head, c], tile(k, c, head)[...]) + factor * nt(tile(g, c, head)[...], pre_bf[head, c])
        ).astype(BF16)

    def k_step(head, c):
        tile(kp, c, head)[...] = flipped(w.at[head, c], tile(q, c, head))

    for part in range(parts + 1):
        grads(part)
        if 0 < part <= STAGES:
            backward.pair(part - 1).start()
        if part > STAGES:
            backward.add_pair(part - STAGES - 1)
    each(result_step)
    each(v_step)
    for stage in range(STAGES):
        each(dscore_step, first=heads // STAGES * stage, last=heads // STAGES * (stage + 1))
        backward.add_chips(stage)
    each(k_step)
    each(q_step)
    forward.drain()
    for i in range(blocks // NORM_BLOCKS):
        for step in range(1, zs):
            norm_copy(i, step).wait_send()

    def suffixes(part):
        for i in range(per):
            head = order[part] + i
            state = backward.carry[head]
            for c in up:
                sfx[head, c] = (factor * (state + pre[head, c])).astype(BF16)

    for stage in range(STAGES):
        backward.hand_over(stage)
        suffixes(STAGES + stage)
    for stage in range(STAGES):
        backward.arrive(stage)
        suffixes(stage)
    backward.drain()


def last_kernel(res, qg, kp, vp, k, v, sfx, res_o, qg_o, kg_o, vg_o, kg, vg, sems):
    rows, width = k.shape
    heads, chunks = width // HD, rows // CHUNK
    whole = [pltpu.make_async_copy(res, res_o, sems.at[0, 0]), pltpu.make_async_copy(qg, qg_o, sems.at[1, 0])]
    for copy in whole:
        copy.start()

    def leave(which, c):
        src, dst = ((kg, kg_o), (vg, vg_o))[which]
        at = pl.ds(c * CHUNK, CHUNK)
        return pltpu.make_async_copy(src.at[at], dst.at[at], sems.at[2 + which, c])

    for c in range(chunks):
        for head in range(heads):
            state = sfx[head, c]
            tile(kg, c, head)[...] = (tile(kp, c, head)[...] + nt(tile(v, c, head)[...], state)).astype(BF16)
            tile(vg, c, head)[...] = (tile(vp, c, head)[...] + nn(tile(k, c, head)[...], state)).astype(BF16)
        leave(0, c).start()
        leave(1, c).start()
    for copy in whole:
        copy.wait()
    for c in range(chunks):
        leave(0, c).wait()
        leave(1, c).wait()


def on_device(queries, keys, values, out_grad):
    rows, width = queries.shape
    heads, chunks, sums = width // HD, rows // CHUNK, rows // (SUB * NORM_BLOCKS)
    chips, zs = lax.axis_size("seq") // 2, lax.axis_size("head")
    dma = pltpu.SemaphoreType.DMA
    flat, flat32 = pltpu.VMEM((rows, width), BF16), pltpu.VMEM((rows, width), F32)
    in_hbm = pl.BlockSpec(memory_space=pltpu.HBM)
    in_vmem = pl.BlockSpec(memory_space=pltpu.VMEM)
    pair = rows * heads * HD * HD * 2
    held = pl.pallas_call(
        main_kernel,
        out_shape=(flat, flat, flat32, flat32, flat, flat, pltpu.VMEM((heads, chunks, HD, HD), BF16)),
        in_specs=[in_hbm] * 4,
        out_specs=[in_vmem] * 7,
        scratch_shapes=[
            flat,
            flat,
            pltpu.VMEM((heads, chunks, CHUNK, CHUNK), BF16),
            pltpu.VMEM((heads, chunks, HD, HD), F32),
            pltpu.VMEM((heads, chunks, HD, HD), BF16),
            pltpu.VMEM((rows, HD), F32),
            pltpu.VMEM((rows, HD), F32),
            pltpu.VMEM((sums, 2 * NORM_BLOCKS, SUB), F32),
            pltpu.VMEM((zs - 1, sums, 2 * NORM_BLOCKS, SUB), F32),
            dma((4, 2 * STAGES)),
            dma((zs - 1, sums)),
            dma((zs - 1, sums)),
        ]
        + scan_scratch(heads, chips)
        + scan_scratch(heads, chips),
        compiler_params=pltpu.CompilerParams(
            collective_id=0, has_side_effects=True, vmem_limit_bytes=27 * MIB
        ),
        cost_estimate=pl.CostEstimate(flops=10 * pair, bytes_accessed=8 * rows * width, transcendentals=0),
        name="attention",
    )(queries, keys, values, out_grad)
    held = [pltpu.with_memory_space_constraint(x, pltpu.VMEM) for x in held]
    like = jax.ShapeDtypeStruct((rows, width), BF16)
    return pl.pallas_call(
        last_kernel,
        out_shape=(like,) * 4,
        in_specs=[in_vmem] * 7,
        out_specs=[in_hbm] * 4,
        scratch_shapes=[flat, flat, dma((4, chunks))],
        compiler_params=pltpu.CompilerParams(vmem_limit_bytes=12 * MIB),
        cost_estimate=pl.CostEstimate(flops=2 * pair, bytes_accessed=8 * rows * width, transcendentals=0),
        name="suffix_gradients",
    )(*held)


def solution(mesh):
    spec = P("seq", "head")
    return jax.shard_map(on_device, mesh=mesh, in_specs=(spec,) * 4, out_specs=(spec,) * 4, check_vma=False)
```
